512 devices in a mesh: grp: 8 (over y, core), dom: 64 (over x, z).
Axes of the slice: x: 4, y: 4, z: 16, core: 2. Of those that a mesh axis runs over, the one named last changes fastest.
Arguments:
- positions: float32 [16384, 3, 128], P(('grp', 'dom')), may hold values from 0 to 1
- masses: float32 [16384, 128], P(('grp', 'dom')), may hold values from 0.5 to 2
- velocities: float32 [16384, 3, 128], P(('grp', 'dom')), may hold values from -3 to 3
- dest_dom: int32 [16384], P(('grp', 'dom')), may hold values from 0 to 63, as said below
- local_pairs: int32 [16384, 4], P(('grp', 'dom')), may hold values from 0 to 31
- export_list: int32 [2560, 4], P(('grp', 'dom')), may hold values from 0 to 31
- cross_pairs: int32 [10240, 4], P(('grp', 'dom')), may hold values from 0 to 31
Outputs:
- positions_out: float32 [16384, 3, 128], P(('grp', 'dom'))
- velocities_out: float32 [16384, 3, 128], P(('grp', 'dom'))
The draws below stay inside these ranges and needn't reach their ends.
Inputs may be any that keep to these rules, and one draw needn't show every extreme that they name: `dest_dom`: every device receives exactly 32 blocks; no device sends more than 2 blocks to one device, and in every group some device sends exactly 2 to one device. Inside a group every device sends equally many blocks to the device a given cyclic distance away along dom.
All inputs are finite; a program needn't handle non-finite values.
Results may differ from the reference program's by a relative error of at most 0.0003.
Values sent between devices are 32-bit elements; how exact they have to be, the bound alone decides.
A program may use at most 64 MiB of HBM per device.

```python
import math
import jax
import jax.numpy as jnp
from jax import lax

BLOCK = 128
BLOCKS_DEV = 32
NEAR = 4
ROUNDS = 5
EXPORTS = 4
FAR = 4
CAPACITY = 2
BLOCKS = 16384
N_GRP = 8
N_DOM = 64


def draw_dest_dom(key, part):
    group_keys = jax.random.split(jax.random.fold_in(key, 17), N_GRP)

    def one_group(group_key):
        offset_key, counts_key, device_key = jax.random.split(group_key, 3)
        offsets = jax.random.permutation(offset_key, N_DOM).astype(jnp.int32)
        first = jax.random.randint(counts_key, (N_DOM,), 1, CAPACITY + 1).astype(jnp.int32)
        first = first.at[0].set(CAPACITY)
        before = jnp.cumsum(first) - first
        base = jnp.clip(BLOCKS_DEV - before, 0, first)
        remaining = BLOCKS_DEV - jnp.sum(base)
        spare = CAPACITY - base
        spare_before = jnp.cumsum(spare) - spare
        extra = jnp.clip(remaining - spare_before, 0, spare)
        counts = base + extra
        ends = jnp.cumsum(counts)
        position = jnp.arange(BLOCKS_DEV, dtype=jnp.int32)
        klass = jnp.sum((position[:, None] >= ends[None, :]).astype(jnp.int32), axis=1)
        offset_of = offsets[klass]

        def one_device(single_key, domain_index):
            ordering = jax.random.permutation(single_key, BLOCKS_DEV)
            return ((domain_index + offset_of[ordering]) % N_DOM).astype(jnp.int32)
        device_keys = jax.random.split(device_key, N_DOM)
        return jax.vmap(one_device)(device_keys, jnp.arange(N_DOM, dtype=jnp.int32)).reshape(-1)
    return jax.vmap(one_group)(group_keys).reshape(-1).astype(jnp.int32)


def plant(drawn, stream_key, smallest, largest):
    shape = drawn.shape
    place = [jax.random.randint(jax.random.fold_in(stream_key, axis), (), 0, shape[axis]) for axis in range(len(shape))]
    drawn = drawn.at[tuple(place)].set(smallest)
    longest = shape.index(max(shape))
    place[longest] = (place[longest] + 1) % shape[longest]
    return drawn.at[tuple(place)].set(largest)


def block_levels(own_key, dims, cuts, low, largest):
    loudness, own = 1.0, jax.random.fold_in(own_key, 6)
    for dim, blocks in cuts:
        steps = jnp.exp(jax.random.uniform(jax.random.fold_in(own, dim), (blocks,), jnp.float32, low / len(cuts), largest / len(cuts)))
        loudness = loudness * jnp.repeat(steps, dims[dim] // blocks).reshape([-1 if axis == dim else 1 for axis in range(len(dims))])
    return loudness


def centred(own_key, dims, scale, reach, pieces=(), kind=jnp.bfloat16):
    drawn = scale * jax.random.normal(own_key, dims, jnp.float32)
    if pieces:
        drawn = drawn * block_levels(own_key, dims, pieces, -0.22, 0.18)
    return jnp.clip(drawn, -reach, reach).astype(kind)


def setup_inputs(seed: int = 0) -> dict:
    arg_keys = jax.random.split(jax.random.key(seed), 8)
    positions = jnp.clip(1.0 * jax.random.uniform(arg_keys[0], (BLOCKS, 3, BLOCK), jnp.float32) ** block_levels(arg_keys[0], (BLOCKS, 3, BLOCK), ((0, 512),), -0.2, 0.2), 0.0, 1.0)
    masses = jnp.clip(jnp.exp(math.log(2.0) - 1.3862944 * jax.random.uniform(arg_keys[1], (BLOCKS, BLOCK), jnp.float32) ** block_levels(arg_keys[1], (BLOCKS, BLOCK), ((0, 512),), -0.2, 0.2)), 0.5, 2.0)
    velocities = centred(arg_keys[2], (BLOCKS, 3, BLOCK), 0.5, 3.0, ((0, 512),), jnp.float32)
    dest_dom = draw_dest_dom(jax.random.fold_in(arg_keys[7], 71), 0)
    local_pairs = plant(jax.random.randint(arg_keys[4], (BLOCKS, NEAR), 0, BLOCKS_DEV), jax.random.fold_in(arg_keys[4], 1), 0, BLOCKS_DEV - 1).astype(jnp.int32)
    export_list = plant(jax.random.randint(arg_keys[5], (N_GRP * N_DOM * ROUNDS, EXPORTS), 0, BLOCKS_DEV), jax.random.fold_in(arg_keys[5], 1), 0, BLOCKS_DEV - 1).astype(jnp.int32)
    cross_pairs = plant(jax.random.randint(arg_keys[6], (N_GRP * N_DOM * ROUNDS * EXPORTS, FAR), 0, BLOCKS_DEV), jax.random.fold_in(arg_keys[6], 1), 0, BLOCKS_DEV - 1).astype(jnp.int32)
    return dict(positions=positions, masses=masses, velocities=velocities, dest_dom=dest_dom, local_pairs=local_pairs, export_list=export_list, cross_pairs=cross_pairs)


GRAVITY = 0.01
SOFTENING = 0.05
SPLIT_SCALE = 0.3
TIMESTEP = 0.5

def block_accel(target_pos, source_pos, source_mass):
    separation = source_pos[:, :, None, :] - target_pos[None, :, :, None]
    distance_sq = lax.optimization_barrier(jnp.sum(separation * separation, axis=1))
    distance = jnp.sqrt(distance_sq)
    softened = distance_sq + SOFTENING * SOFTENING
    inverse = 1.0 / (softened * jnp.sqrt(softened))
    scaled = distance / (2.0 * SPLIT_SCALE)
    shaping = lax.erfc(scaled) + distance / (SPLIT_SCALE * math.sqrt(math.pi)) * jnp.exp(-scaled * scaled)
    weight = source_mass[:, None, :] * shaping * inverse
    return GRAVITY * lax.optimization_barrier(jnp.sum(separation * weight[:, None, :, :], axis=(0, 3)))

def local_accel(new_pos, new_mass, local_pairs):
    block_count = new_pos.shape[0]
    batch_width = 4
    groups = block_count // batch_width
    near_pos = new_pos[local_pairs]
    near_mass = new_mass[local_pairs]

    def batch_step(batch_items):
        return jax.vmap(block_accel)(batch_items[0], batch_items[1], batch_items[2])
    shaped = (new_pos.reshape((groups, batch_width) + new_pos.shape[1:]), near_pos.reshape((groups, batch_width) + near_pos.shape[1:]), near_mass.reshape((groups, batch_width) + near_mass.shape[1:]))
    return lax.map(batch_step, shaped).reshape(new_pos.shape)

def reference(positions, masses, velocities, dest_dom, local_pairs, export_list, cross_pairs):
    devices = N_GRP * N_DOM
    group_blocks = N_DOM * BLOCKS_DEV

    def migrate_group(targets):
        one_hot = (targets[:, None] == jnp.arange(N_DOM, dtype=jnp.int32)[None, :]).astype(jnp.int32)
        rank_in_peer = lax.optimization_barrier(jnp.sum((jnp.cumsum(one_hot, axis=0) - one_hot) * one_hot, axis=1))
        return (targets * BLOCKS_DEV + rank_in_peer).astype(jnp.int32)
    new_slot = jax.vmap(migrate_group)(dest_dom.reshape(N_GRP, group_blocks))
    new_slot = (new_slot + (jnp.arange(N_GRP, dtype=jnp.int32) * group_blocks)[:, None]).reshape(-1).astype(jnp.int32)
    new_pos = jnp.zeros_like(positions).at[new_slot].set(positions)
    new_mass = jnp.zeros_like(masses).at[new_slot].set(masses)
    new_vel = jnp.zeros_like(velocities).at[new_slot].set(velocities)
    dev_pos = new_pos.reshape(devices, BLOCKS_DEV, 3, BLOCK)
    dev_mass = new_mass.reshape(devices, BLOCKS_DEV, BLOCK)
    pairs = local_pairs.reshape(devices, BLOCKS_DEV, NEAR)
    acceleration = lax.map(lambda parts: local_accel(parts[0], parts[1], parts[2]), (dev_pos, dev_mass, pairs))
    exports = export_list.reshape(devices, ROUNDS, EXPORTS)
    crosses = cross_pairs.reshape(devices, ROUNDS, EXPORTS, FAR)
    bit_count = devices.bit_length() - 1
    device_ids = jnp.arange(devices, dtype=jnp.int32)
    for phase_number in range(ROUNDS):
        bit_number = phase_number * bit_count // ROUNDS

        def remote(device_id, phase_number=phase_number, bit_number=bit_number):
            partner = jnp.bitwise_xor(device_id, jnp.int32(1 << bit_number))
            targets = dev_pos[device_id][exports[device_id, phase_number]]
            sources = crosses[partner, phase_number]
            return jax.vmap(block_accel)(targets, dev_pos[partner][sources], dev_mass[partner][sources])
        contribution = lax.map(remote, device_ids)
        acceleration = acceleration.at[device_ids[:, None], exports[:, phase_number]].add(contribution)
    acceleration = acceleration.reshape(new_vel.shape)
    velocities_out = new_vel + TIMESTEP * acceleration
    positions_out = new_pos + TIMESTEP * velocities_out
    return (positions_out, velocities_out)
```

```python
import functools
import math

import jax
import jax.numpy as jnp
from jax import lax
from jax.experimental import pallas as pl
from jax.experimental.pallas import tpu as pltpu
from jax.sharding import PartitionSpec as P

BLOCK = 128
SLOTS = 32
NEAR = 4
ROUNDS = 5
EXPORTS = 4
FAR = 4
TIMESTEP = 0.5
F32, BF16 = jnp.float32, jnp.bfloat16
MESH = pl.DeviceIdType.MESH

ALPHA = math.log2(math.e) / 0.36
SOFT = ALPHA * 0.05**2
N0, N1, N2, N3 = 8.53126995, 11.49321071, 11.59229692, 5.3254959
D0, D1, D2 = 8.01883474, 10.80288261, 5.33752372
LEAD = 0.9399344975074229
SCALE = 0.01 * ALPHA**1.5 * LEAD
KEEP = 48
LATE = 12


def split3(x):
    first = x.astype(BF16).astype(F32)
    rest = x - first
    second = rest.astype(BF16).astype(F32)
    return first, second, rest - second


def exact_dot(choice, values):
    total = None
    for piece in split3(values):
        part = jnp.dot(choice, piece.astype(BF16), preferred_element_type=F32)
        total = part if total is None else total + part
    return total


def weight(raw):
    v = jnp.maximum(raw, 1e-30)
    u = v * lax.rsqrt(v)
    t = v + SOFT
    upper = (((u + N3) * u + N2) * u + N1) * u + N0
    lower = ((u + D2) * u + D1) * u + D0
    p = t * lower * jnp.exp2(v)
    return upper * lax.rsqrt(p * p * t)


def target_rows(x):
    row = lax.broadcasted_iota(jnp.int32, (8, BLOCK), 0)
    x = jnp.where(row < 3, x - 0.5, 0.0)
    norm = ALPHA * jnp.sum(x * x, axis=0, keepdims=True)
    own = jnp.where(row < 3, x, jnp.where(row == 3, norm, jnp.where(row == 4, 1.0, 0.0)))
    t1, t2, t3 = split3(own)
    return jnp.concatenate([t1, t2, t1, t2, t3, t1], axis=0).astype(BF16)


def source_rows(x):
    row = lax.broadcasted_iota(jnp.int32, (8, BLOCK), 0)
    mass = x[3:4]
    x = jnp.where(row < 3, x - 0.5, 0.0)
    norm = ALPHA * jnp.sum(x * x, axis=0, keepdims=True)
    own = jnp.where(row < 3, (-2.0 * ALPHA) * x, jnp.where(row == 3, 1.0, jnp.where(row == 4, norm, 0.0)))
    s1, s2, s3 = split3(own)
    moment = (SCALE * mass) * jnp.where(row < 3, x, jnp.where(row == 3, 1.0, 0.0))
    m1, m2, m3 = split3(moment)
    return (
        jnp.concatenate([s1, s1, s2, s2, s1, s3], axis=0),
        jnp.concatenate([m1, m2, m3, jnp.zeros_like(m1)], axis=0).astype(BF16),
    )


def pair_sum(x, features, source_ids, src, mom):
    highs, lows, moments = [], [], []
    for s in source_ids:
        raw = jnp.dot(src[s][:, :KEEP], features, preferred_element_type=F32)
        w = weight(raw)
        high = w.astype(BF16)
        highs.append(high)
        lows.append((w - high.astype(F32)).astype(BF16))
        moments.append(mom[s])
    moments = jnp.concatenate(moments, axis=1)
    a = jnp.dot(moments, jnp.concatenate(highs, axis=0), preferred_element_type=F32)
    a = a + jnp.dot(moments, jnp.concatenate(lows, axis=0), preferred_element_type=F32)
    a = a[0:8] + a[8:16] + a[16:24]
    return a - (x - 0.5) * a[3:4]


def flipped(index, bit):
    low = 2**bit
    return index + low * (1 - 2 * lax.rem(lax.div(index, low), 2))


def kernel(
    domains, bits, pos, mass, vel, dest, near_ids, export_ids, far_ids, pos_out, vel_out,
    pack_p, land_p, pack_v, land_v, new, tgt, src, mom, acc, out_x, in_x, out_a, in_a,
    move_send, move_recv, x_send, x_recv, a_send, a_recv,
):
    grp, dom = lax.axis_index("grp"), lax.axis_index("dom")
    inner = domains.bit_length() - 1

    def partner(bit):
        return (grp, flipped(dom, bit)) if bit < inner else (flipped(grp, bit - inner), dom)

    def peer(step):
        return (grp, lax.rem(dom + step, domains))

    barrier = pltpu.get_barrier_semaphore()
    outer = [bit for bit in bits if bit >= inner]

    @pl.loop(1, domains)
    def _(step):
        pl.semaphore_signal(barrier, inc=1, device_id=peer(step), device_id_type=MESH)

    for bit in outer:
        pl.semaphore_signal(barrier, inc=1, device_id=partner(bit), device_id_type=MESH)

    lane = lax.broadcasted_iota(jnp.int32, (1, BLOCK), 1)
    owner = lax.rem(lane, SLOTS)
    target = jnp.zeros((1, BLOCK), jnp.int32)
    for b in range(SLOTS):
        target = jnp.where(owner == b, dest[b], target)
    rows = lax.broadcasted_iota(jnp.int32, (SLOTS, BLOCK), 0)
    lanes = lax.broadcasted_iota(jnp.int32, (SLOTS, BLOCK), 1)
    owners = lax.rem(lanes, SLOTS)

    def as_column(row):
        return jnp.sum(jnp.where(lanes == rows, row, 0.0), axis=1, keepdims=True)

    target_f = target.astype(F32)
    same = (as_column(target_f) == target_f) & (rows < owners)
    rank = jnp.sum(jnp.where(same, 1.0, 0.0), axis=0, keepdims=True)
    away = lax.rem(target - dom + domains, domains)
    away_f = away.astype(F32)
    base = away_f * 8.0 + rank * 4.0
    came_from = lax.rem(dom - away + domains, domains).astype(F32) * 2.0 + rank
    place = jnp.sum(jnp.where(as_column(came_from) < came_from, 1.0, 0.0), axis=0, keepdims=True)

    def packed(stacked):
        key = base + lax.div(lane, SLOTS).astype(F32)
        count = lax.broadcasted_iota(jnp.int32, (domains * 8, BLOCK), 0).astype(F32)
        choice = jnp.where(count == key, 1.0, 0.0).astype(BF16)
        return exact_dot(choice, stacked).reshape(domains, 8, BLOCK)

    row8 = lax.broadcasted_iota(jnp.int32, (SLOTS * 8, BLOCK), 0)
    lane8 = lax.broadcasted_iota(jnp.int32, (SLOTS * 8, BLOCK), 1)
    found = (lane8 < SLOTS) & (place == lax.div(row8, 8).astype(F32))
    key = jnp.sum(jnp.where(found, base, 0.0), axis=1, keepdims=True)
    part = lax.rem(lax.broadcasted_iota(jnp.int32, (SLOTS * 8, 1), 0), 8)
    key = jnp.where(part < 4, key + part.astype(F32), -1.0)

    def unpacked(land):
        count = lax.broadcasted_iota(jnp.int32, (SLOTS * 8, domains * 8), 1).astype(F32)
        choice = jnp.where(count == key, 1.0, 0.0).astype(BF16)
        return exact_dot(choice, land.reshape(domains * 8, BLOCK)).reshape(SLOTS, 8, BLOCK)

    pack_p[...] = packed(jnp.concatenate([pos[:, 0], pos[:, 1], pos[:, 2], mass[...]], axis=0))
    pack_v[...] = packed(
        jnp.concatenate([vel[:, 0], vel[:, 1], vel[:, 2], jnp.zeros((SLOTS, BLOCK), F32)], axis=0)
    )
    pl.semaphore_wait(barrier, domains - 1 + len(outer))

    def move(pack, land, k):
        @pl.loop(1, domains)
        def _(step):
            pltpu.make_async_remote_copy(
                src_ref=pack.at[step], dst_ref=land.at[step],
                send_sem=move_send.at[k], recv_sem=move_recv.at[k],
                device_id=peer(step), device_id_type=MESH,
            ).start()

    def moved(pack, land, k):
        return pltpu.make_async_remote_copy(
            src_ref=pack.at[pl.ds(1, domains - 1)], dst_ref=land.at[pl.ds(1, domains - 1)],
            send_sem=move_send.at[k], recv_sem=move_recv.at[k],
            device_id=peer(1), device_id_type=MESH,
        )

    move(pack_p, land_p, 0)
    move(pack_v, land_v, 1)
    land_p[0] = pack_p[0]
    land_v[0] = pack_v[0]
    moved(pack_p, land_p, 0).wait_recv()
    new[...] = unpacked(land_p[...])

    def visit(r):
        return pltpu.make_async_remote_copy(
            src_ref=out_x.at[r], dst_ref=in_x.at[r], send_sem=x_send.at[r], recv_sem=x_recv.at[r],
            device_id=partner(bits[r]), device_id_type=MESH,
        )

    def give_back(r):
        return pltpu.make_async_remote_copy(
            src_ref=out_a.at[r], dst_ref=in_a.at[r], send_sem=a_send.at[r], recv_sem=a_recv.at[r],
            device_id=partner(bits[r]), device_id_type=MESH,
        )

    for r in range(ROUNDS):
        for e in range(EXPORTS):
            out_x[r, e] = new[export_ids[r, e]]
        visit(r).start()

    def prepare(b, carry):
        x = new[b]
        tgt[b] = target_rows(x)
        features, moments = source_rows(x)
        src[b] = jnp.concatenate([features, jnp.zeros((BLOCK - KEEP, BLOCK), F32)], axis=0).T.astype(BF16)
        mom[b] = moments
        return carry

    lax.fori_loop(0, SLOTS, prepare, 0, unroll=4)

    def near(b, carry):
        acc[b] = pair_sum(new[b], tgt[b], [near_ids[b, k] for k in range(NEAR)], src, mom)
        return carry

    lax.fori_loop(0, SLOTS - LATE, near, 0, unroll=4)
    for r in range(ROUNDS):
        visit(r).wait_recv()

        def far(e, carry, r=r):
            x = in_x[r, e]
            ids = [far_ids[r * EXPORTS + e, k] for k in range(FAR)]
            out_a[r, e] = pair_sum(x, target_rows(x), ids, src, mom)
            return carry

        lax.fori_loop(0, EXPORTS, far, 0, unroll=4)
        give_back(r).start()
    lax.fori_loop(SLOTS - LATE, SLOTS, near, 0, unroll=4)

    moved(pack_v, land_v, 1).wait_recv()
    new_vel = unpacked(land_v[...])
    wide = lax.broadcasted_iota(jnp.int32, (1, 256), 1)
    slot = jnp.full((1, 256), -1, jnp.int32)
    for r in range(ROUNDS):
        give_back(r).wait_recv()
        for e in range(EXPORTS):
            slot = jnp.where(lax.div(wide, 8) == r * EXPORTS + e, export_ids[r, e], slot)
    rows8 = lax.broadcasted_iota(jnp.int32, (SLOTS * 8, 256), 0)
    wide8 = lax.broadcasted_iota(jnp.int32, (SLOTS * 8, 256), 1)
    hit = (lax.div(rows8, 8) == slot) & (lax.rem(rows8, 8) == lax.rem(wide8, 8))
    returned = jnp.concatenate(
        [in_a[...].reshape(ROUNDS * EXPORTS * 8, BLOCK), jnp.zeros((256 - ROUNDS * EXPORTS * 8, BLOCK), F32)], axis=0
    )
    far_acc = exact_dot(jnp.where(hit, 1.0, 0.0).astype(BF16), returned).reshape(SLOTS, 8, BLOCK)
    new_vel = new_vel + TIMESTEP * (acc[...] + far_acc)
    new_pos = new[...] + TIMESTEP * new_vel
    pos_out[...] = new_pos[:, :3]
    vel_out[...] = new_vel[:, :3]
    for r in range(ROUNDS):
        visit(r).wait_send()
        give_back(r).wait_send()
    moved(pack_p, land_p, 0).wait_send()
    moved(pack_v, land_v, 1).wait_send()


def on_device(positions, masses, velocities, dest_dom, local_pairs, export_list, cross_pairs):
    domains = lax.axis_size("dom")
    devices = domains * lax.axis_size("grp")
    levels = devices.bit_length() - 1
    bits = [r * levels // ROUNDS for r in range(ROUNDS)]
    vmem, smem = pl.BlockSpec(memory_space=pltpu.VMEM), pl.BlockSpec(memory_space=pltpu.SMEM)
    moves = pltpu.VMEM((domains, 8, BLOCK), F32)
    visits = pltpu.VMEM((ROUNDS, EXPORTS, 8, BLOCK), F32)
    return pl.pallas_call(
        functools.partial(kernel, domains, bits),
        out_shape=(
            jax.ShapeDtypeStruct(positions.shape, F32),
            jax.ShapeDtypeStruct(velocities.shape, F32),
        ),
        in_specs=[vmem] * 3 + [smem] * 4,
        out_specs=(vmem, vmem),
        scratch_shapes=[
            moves, moves, moves, moves,
            pltpu.VMEM((SLOTS, 8, BLOCK), F32),
            pltpu.VMEM((SLOTS, KEEP, BLOCK), BF16),
            pltpu.VMEM((SLOTS, BLOCK, BLOCK), BF16),
            pltpu.VMEM((SLOTS, 32, BLOCK), BF16),
            pltpu.VMEM((SLOTS, 8, BLOCK), F32),
            visits, visits, visits, visits,
            pltpu.SemaphoreType.DMA((2,)), pltpu.SemaphoreType.DMA((2,)),
            pltpu.SemaphoreType.DMA((ROUNDS,)), pltpu.SemaphoreType.DMA((ROUNDS,)),
            pltpu.SemaphoreType.DMA((ROUNDS,)), pltpu.SemaphoreType.DMA((ROUNDS,)),
        ],
        compiler_params=pltpu.CompilerParams(
            collective_id=0, has_side_effects=True, vmem_limit_bytes=40 * 2**20
        ),
    )(positions, masses, velocities, dest_dom, local_pairs, export_list, cross_pairs)


def solution(mesh):
    both = ("grp", "dom")
    return jax.shard_map(
        on_device,
        mesh=mesh,
        in_specs=(
            P(both, None, None), P(both, None), P(both, None, None), P(both), P(both, None), P(both, None), P(both, None),
        ),
        out_specs=(P(both, None, None), P(both, None, None)),
        check_vma=False,
    )
```

```python
import functools
import math

import jax
import jax.numpy as jnp
from jax import lax
from jax.experimental import pallas as pl
from jax.experimental.pallas import tpu as pltpu
from jax.sharding import PartitionSpec as P

BLOCK = 128
SLOTS = 32
NEAR = 4
ROUNDS = 5
EXPORTS = 4
FAR = 4
TIMESTEP = 0.5
F32, BF16 = jnp.float32, jnp.bfloat16
MESH = pl.DeviceIdType.MESH

ALPHA = 4.009245535636174
SOFT = ALPHA * 0.05**2
N0, N1, N2, N3 = 638.3696617050974, 622.7581356810975, 614.039653607777, 155.2143515804912
D0, D1 = 3.7186906578024175, 3.627694577131586
LEAD = 0.005825292410791371
SCALE = 0.01 * ALPHA**1.5 * LEAD * 2.0**SOFT
KEEP = 48
LATE = 12


def split3(x):
    first = x.astype(BF16).astype(F32)
    rest = x - first
    second = rest.astype(BF16).astype(F32)
    return first, second, rest - second


def exact_dot(choice, values):
    total = None
    for piece in split3(values):
        part = jnp.dot(choice, piece.astype(BF16), preferred_element_type=F32)
        total = part if total is None else total + part
    return total


def weight(t):
    v = jnp.maximum(t - SOFT, 1e-30)
    u = v * lax.rsqrt(v)
    upper = (((u + N3) * u + N2) * u + N1) * u + N0
    lower = (u + D1) * u + D0
    p = t * (lower * jnp.exp2(t))
    return upper * lax.rsqrt(p * p * t)


def target_rows(x):
    row = lax.broadcasted_iota(jnp.int32, (8, BLOCK), 0)
    x = jnp.where(row < 3, x - 0.5, 0.0)
    norm = ALPHA * jnp.sum(x * x, axis=0, keepdims=True)
    own = jnp.where(row < 3, x, jnp.where(row == 3, norm + SOFT, jnp.where(row == 4, 1.0, 0.0)))
    t1, t2, t3 = split3(own)
    return jnp.concatenate([t1, t2, t1, t2, t3, t1], axis=0).astype(BF16)


def source_rows(x):
    row = lax.broadcasted_iota(jnp.int32, (8, BLOCK), 0)
    mass = x[3:4]
    x = jnp.where(row < 3, x - 0.5, 0.0)
    norm = ALPHA * jnp.sum(x * x, axis=0, keepdims=True)
    own = jnp.where(row < 3, (-2.0 * ALPHA) * x, jnp.where(row == 3, 1.0, jnp.where(row == 4, norm, 0.0)))
    s1, s2, s3 = split3(own)
    moment = (SCALE * mass) * jnp.where(row < 3, x, jnp.where(row == 3, 1.0, 0.0))
    m1, m2, m3 = split3(moment)
    moments = jnp.concatenate([m1, m2, m3, jnp.zeros_like(m1)], axis=0).astype(BF16)
    return jnp.concatenate([s1, s1, s2, s2, s1, s3], axis=0), jnp.concatenate([moments, moments], axis=1)


def pair_sum(x, features, source_ids, src, mom):
    sources = jnp.concatenate([src[s] for s in source_ids], axis=0)[:, :KEEP]
    softened = jnp.dot(sources, features, preferred_element_type=F32)
    a = None
    for k, s in enumerate(source_ids):
        w = weight(softened[k * BLOCK : (k + 1) * BLOCK])
        high = w.astype(BF16)
        low = (w - high.astype(F32)).astype(BF16)
        part = jnp.dot(mom[s], jnp.concatenate([high, low], axis=0), preferred_element_type=F32)
        a = part if a is None else a + part
    a = a[0:8] + a[8:16] + a[16:24]
    return a - (x - 0.5) * a[3:4]


def flipped(index, bit):
    low = 2**bit
    return index + low * (1 - 2 * lax.rem(lax.div(index, low), 2))


def kernel(
    domains, bits, pos_in, mass_in, vel_in, dest, near_ids, export_ids, far_ids, pos_out, vel_out, acc_out,
    pos, mass, vel, pack_p, land_p, pack_v, land_v, held_v, new, tgt, src, mom, acc, out_x, in_x, out_a, in_a,
    move_send, move_recv, x_send, x_recv, a_send, a_recv, load,
):
    grp, dom = lax.axis_index("grp"), lax.axis_index("dom")
    inner = domains.bit_length() - 1

    def partner(bit):
        return (grp, flipped(dom, bit)) if bit < inner else (flipped(grp, bit - inner), dom)

    def peer(step):
        return (grp, lax.rem(dom + step, domains))

    barrier = pltpu.get_barrier_semaphore()
    outer = [bit for bit in bits if bit >= inner]

    @pl.loop(1, domains, unroll=9)
    def _(step):
        pl.semaphore_signal(barrier, inc=1, device_id=peer(step), device_id_type=MESH)

    for bit in outer:
        pl.semaphore_signal(barrier, inc=1, device_id=partner(bit), device_id_type=MESH)

    loads = [
        pltpu.make_async_copy(given, held, load.at[i])
        for i, (given, held) in enumerate(((pos_in, pos), (mass_in, mass), (vel_in, vel)))
    ]
    for copy in loads:
        copy.start()

    lane = lax.broadcasted_iota(jnp.int32, (1, BLOCK), 1)
    owner = lax.rem(lane, SLOTS)
    target = jnp.zeros((1, BLOCK), jnp.int32)
    for b in range(SLOTS):
        target = jnp.where(owner == b, dest[b], target)
    rows = lax.broadcasted_iota(jnp.int32, (SLOTS, BLOCK), 0)
    lanes = lax.broadcasted_iota(jnp.int32, (SLOTS, BLOCK), 1)
    owners = lax.rem(lanes, SLOTS)

    def as_column(row):
        return jnp.sum(jnp.where(lanes == rows, row, 0.0), axis=1, keepdims=True)

    target_f = target.astype(F32)
    same = (as_column(target_f) == target_f) & (rows < owners)
    rank = jnp.sum(jnp.where(same, 1.0, 0.0), axis=0, keepdims=True)
    away = lax.rem(target - dom + domains, domains)
    away_f = away.astype(F32)
    base = away_f * 8.0 + rank * 4.0
    came_from = lax.rem(dom - away + domains, domains).astype(F32) * 2.0 + rank
    place = jnp.sum(jnp.where(as_column(came_from) < came_from, 1.0, 0.0), axis=0, keepdims=True)

    def packed(stacked):
        key = base + lax.div(lane, SLOTS).astype(F32)
        count = lax.broadcasted_iota(jnp.int32, (domains * 8, BLOCK), 0).astype(F32)
        choice = jnp.where(count == key, 1.0, 0.0).astype(BF16)
        return exact_dot(choice, stacked).reshape(domains, 8, BLOCK)

    row8 = lax.broadcasted_iota(jnp.int32, (SLOTS * 8, BLOCK), 0)
    lane8 = lax.broadcasted_iota(jnp.int32, (SLOTS * 8, BLOCK), 1)
    found = (lane8 < SLOTS) & (place == lax.div(row8, 8).astype(F32))
    key = jnp.sum(jnp.where(found, base, 0.0), axis=1, keepdims=True)
    part = lax.rem(lax.broadcasted_iota(jnp.int32, (SLOTS * 8, 1), 0), 8)
    key = jnp.where(part < 4, key + part.astype(F32), -1.0)

    def unpacked(land):
        count = lax.broadcasted_iota(jnp.int32, (SLOTS * 8, domains * 8), 1).astype(F32)
        choice = jnp.where(count == key, 1.0, 0.0).astype(BF16)
        return exact_dot(choice, land.reshape(domains * 8, BLOCK)).reshape(SLOTS, 8, BLOCK)

    for copy in loads:
        copy.wait()
    pack_p[...] = packed(jnp.concatenate([pos[0], pos[1], pos[2], mass[...]], axis=0))
    pl.semaphore_wait(barrier, domains - 1 + len(outer))

    def move(pack, land, k):
        @pl.loop(1, domains, unroll=9)
        def _(step):
            pltpu.make_async_remote_copy(
                src_ref=pack.at[step], dst_ref=land.at[step],
                send_sem=move_send.at[k], recv_sem=move_recv.at[k],
                device_id=peer(step), device_id_type=MESH,
            ).start()

    def moved(pack, land, k):
        return pltpu.make_async_remote_copy(
            src_ref=pack.at[pl.ds(1, domains - 1)], dst_ref=land.at[pl.ds(1, domains - 1)],
            send_sem=move_send.at[k], recv_sem=move_recv.at[k],
            device_id=peer(1), device_id_type=MESH,
        )

    move(pack_p, land_p, 0)
    pack_v[...] = packed(
        jnp.concatenate([vel[0], vel[1], vel[2], jnp.zeros((SLOTS, BLOCK), F32)], axis=0)
    )
    land_p[0] = pack_p[0]
    land_v[0] = pack_v[0]
    moved(pack_p, land_p, 0).wait_recv()
    new[...] = unpacked(land_p[...])

    def visit(r):
        return pltpu.make_async_remote_copy(
            src_ref=out_x.at[r], dst_ref=in_x.at[r], send_sem=x_send.at[r], recv_sem=x_recv.at[r],
            device_id=partner(bits[r]), device_id_type=MESH,
        )

    def give_back(r):
        return pltpu.make_async_remote_copy(
            src_ref=out_a.at[r], dst_ref=in_a.at[r], send_sem=a_send.at[r], recv_sem=a_recv.at[r],
            device_id=partner(bits[r]), device_id_type=MESH,
        )

    for r in range(ROUNDS):
        for e in range(EXPORTS):
            out_x[r, e] = new[export_ids[e, r]]
        visit(r).start()

    move(pack_v, land_v, 1)

    def prepare(b, carry):
        x = new[b]
        tgt[b] = target_rows(x)
        features, moments = source_rows(x)
        src[b] = jnp.concatenate([features, jnp.zeros((BLOCK - KEEP, BLOCK), F32)], axis=0).T.astype(BF16)
        mom[b] = moments
        return carry

    lax.fori_loop(0, SLOTS, prepare, 0, unroll=4)

    def near(b, carry):
        acc[b] = pair_sum(new[b], tgt[b], [near_ids[k, b] for k in range(NEAR)], src, mom)
        return carry

    lax.fori_loop(0, SLOTS - LATE, near, 0, unroll=10)
    for r in range(ROUNDS):
        visit(r).wait_recv()

        def far(e, carry, r=r):
            x = in_x[r, e]
            ids = [far_ids[k, r * EXPORTS + e] for k in range(FAR)]
            out_a[r, e] = pair_sum(x, target_rows(x), ids, src, mom)
            return carry

        lax.fori_loop(0, EXPORTS, far, 0, unroll=4)
        give_back(r).start()
    lax.fori_loop(SLOTS - LATE, SLOTS, near, 0, unroll=6)

    moved(pack_v, land_v, 1).wait_recv()
    new_vel = unpacked(land_v[...])
    wide = lax.broadcasted_iota(jnp.int32, (1, 256), 1)
    slot = jnp.full((1, 256), -1, jnp.int32)
    for r in range(ROUNDS):
        give_back(r).wait_recv()
        for e in range(EXPORTS):
            slot = jnp.where(lax.div(wide, 8) == r * EXPORTS + e, export_ids[e, r], slot)
    rows8 = lax.broadcasted_iota(jnp.int32, (SLOTS * 8, 256), 0)
    wide8 = lax.broadcasted_iota(jnp.int32, (SLOTS * 8, 256), 1)
    hit = (lax.div(rows8, 8) == slot) & (lax.rem(rows8, 8) == lax.rem(wide8, 8))
    returned = jnp.concatenate(
        [in_a[...].reshape(ROUNDS * EXPORTS * 8, BLOCK), jnp.zeros((256 - ROUNDS * EXPORTS * 8, BLOCK), F32)], axis=0
    )
    far_acc = exact_dot(jnp.where(hit, 1.0, 0.0).astype(BF16), returned).reshape(SLOTS, 8, BLOCK)
    acc[...] = acc[...] + far_acc
    held_v[...] = new_vel
    for c in range(3):
        pos_out[c] = new[:, c]
        vel_out[c] = held_v[:, c]
        acc_out[c] = acc[:, c]
    for r in range(ROUNDS):
        visit(r).wait_send()
        give_back(r).wait_send()
    moved(pack_p, land_p, 0).wait_send()
    moved(pack_v, land_v, 1).wait_send()


def on_device(positions, masses, velocities, dest_dom, local_pairs, export_list, cross_pairs):
    domains = lax.axis_size("dom")
    devices = domains * lax.axis_size("grp")
    levels = devices.bit_length() - 1
    bits = [r * levels // ROUNDS for r in range(ROUNDS)]
    hbm, vmem = pl.BlockSpec(memory_space=pltpu.HBM), pl.BlockSpec(memory_space=pltpu.VMEM)
    smem = pl.BlockSpec(memory_space=pltpu.SMEM)
    moves = pltpu.VMEM((domains, 8, BLOCK), F32)
    visits = pltpu.VMEM((ROUNDS, EXPORTS, 8, BLOCK), F32)
    across = (1, 0, 2)
    outs = pl.pallas_call(
        functools.partial(kernel, domains, bits),
        out_shape=(jax.ShapeDtypeStruct((3, SLOTS, BLOCK), F32),) * 3,
        in_specs=[hbm] * 3 + [smem] * 4,
        out_specs=(vmem,) * 3,
        scratch_shapes=[
            pltpu.VMEM((3, SLOTS, BLOCK), F32), pltpu.VMEM((SLOTS, BLOCK), F32), pltpu.VMEM((3, SLOTS, BLOCK), F32),
            moves, moves, moves, moves,
            pltpu.VMEM((SLOTS, 8, BLOCK), F32),
            pltpu.VMEM((SLOTS, 8, BLOCK), F32),
            pltpu.VMEM((SLOTS, KEEP, BLOCK), BF16),
            pltpu.VMEM((SLOTS, BLOCK, BLOCK), BF16),
            pltpu.VMEM((SLOTS, 32, 2 * BLOCK), BF16),
            pltpu.VMEM((SLOTS, 8, BLOCK), F32),
            visits, visits, visits, visits,
            pltpu.SemaphoreType.DMA((2,)), pltpu.SemaphoreType.DMA((2,)),
            pltpu.SemaphoreType.DMA((ROUNDS,)), pltpu.SemaphoreType.DMA((ROUNDS,)),
            pltpu.SemaphoreType.DMA((ROUNDS,)), pltpu.SemaphoreType.DMA((ROUNDS,)), pltpu.SemaphoreType.DMA((3,)),
        ],
        compiler_params=pltpu.CompilerParams(
            collective_id=0, has_side_effects=True, vmem_limit_bytes=60 * 2**20
        ),
    )(
        positions.transpose(across), masses, velocities.transpose(across), dest_dom,
        local_pairs.T, export_list.T, cross_pairs.T,
    )
    new_pos, new_vel, acceleration = (out.transpose(across) for out in outs)
    vel_out = new_vel + TIMESTEP * acceleration
    return new_pos + TIMESTEP * vel_out, vel_out


def solution(mesh):
    both = ("grp", "dom")
    return jax.shard_map(
        on_device,
        mesh=mesh,
        in_specs=(
            P(both, None, None), P(both, None), P(both, None, None), P(both), P(both, None), P(both, None), P(both, None),
        ),
        out_specs=(P(both, None, None), P(both, None, None)),
        check_vma=False,
    )
```

```python
import functools
import math

import jax
import jax.numpy as jnp
from jax import lax
from jax.experimental import pallas as pl
from jax.experimental.pallas import tpu as pltpu
from jax.sharding import PartitionSpec as P

BLOCK = 128
SLOTS = 32
NEAR = 4
ROUNDS = 5
EXPORTS = 4
FAR = 4
TIMESTEP = 0.5
F32, BF16 = jnp.float32, jnp.bfloat16
MESH = pl.DeviceIdType.MESH

ALPHA = 4.009245535636174
SOFT = ALPHA * 0.05**2
N0, N1, N2, N3 = 638.3696617050974, 622.7581356810975, 614.039653607777, 155.2143515804912
D0, D1 = 3.7186906578024175, 3.627694577131586
LEAD = 0.005825292410791371
SCALE = 0.01 * ALPHA**1.5 * LEAD * 2.0**SOFT
KEEP = 48
FETCH = 2
ORDER = (3, 1, 4, 0)
LATE = 12


def split3(x):
    first = x.astype(BF16).astype(F32)
    rest = x - first
    second = rest.astype(BF16).astype(F32)
    return first, second, rest - second


def exact_dot(choice, values):
    total = None
    for piece in split3(values):
        part = jnp.dot(choice, piece.astype(BF16), preferred_element_type=F32)
        total = part if total is None else total + part
    return total


def weight(t):
    v = jnp.maximum(t - SOFT, 1e-30)
    u = v * lax.rsqrt(v)
    upper = (((u + N3) * u + N2) * u + N1) * u + N0
    lower = (u + D1) * u + D0
    p = t * (lower * jnp.exp2(t))
    return upper * lax.rsqrt(p * p * t)


def target_rows(x):
    row = lax.broadcasted_iota(jnp.int32, (8, BLOCK), 0)
    x = jnp.where(row < 3, x - 0.5, 0.0)
    norm = ALPHA * jnp.sum(x * x, axis=0, keepdims=True)
    own = jnp.where(row < 3, x, jnp.where(row == 3, norm + SOFT, jnp.where(row == 4, 1.0, 0.0)))
    t1, t2, t3 = split3(own)
    return jnp.concatenate([t1, t2, t1, t2, t3, t1], axis=0).astype(BF16)


def source_rows(x):
    row = lax.broadcasted_iota(jnp.int32, (8, BLOCK), 0)
    mass = x[3:4]
    x = jnp.where(row < 3, x - 0.5, 0.0)
    norm = ALPHA * jnp.sum(x * x, axis=0, keepdims=True)
    own = jnp.where(row < 3, (-2.0 * ALPHA) * x, jnp.where(row == 3, 1.0, jnp.where(row == 4, norm, 0.0)))
    s1, s2, s3 = split3(own)
    moment = (SCALE * mass) * jnp.where(row < 3, x, jnp.where(row == 3, 1.0, 0.0))
    m1, m2, m3 = split3(moment)
    moments = jnp.concatenate([m1, m2, m3, jnp.zeros_like(m1)], axis=0).astype(BF16)
    return jnp.concatenate([s1, s1, s2, s2, s1, s3], axis=0), jnp.concatenate([moments, moments], axis=1)


def pair_sum(x, features, source_ids, src, mom):
    sources = jnp.concatenate([src[s] for s in source_ids], axis=0)[:, :KEEP]
    softened = jnp.dot(sources, features, preferred_element_type=F32)
    a = None
    for k, s in enumerate(source_ids):
        w = weight(softened[k * BLOCK : (k + 1) * BLOCK])
        high = w.astype(BF16)
        low = (w - high.astype(F32)).astype(BF16)
        part = jnp.dot(mom[s], jnp.concatenate([high, low], axis=0), preferred_element_type=F32)
        a = part if a is None else a + part
    a = a[0:8] + a[8:16] + a[16:24]
    return a - (x - 0.5) * a[3:4]


def flipped(index, bit):
    low = 2**bit
    return index + low * (1 - 2 * lax.rem(lax.div(index, low), 2))


def kernel(
    domains, bits, pos_in, mass_in, vel_in, dest, near_ids, export_ids, far_ids, pos_out, vel_out, acc_out,
    pos, mass, vel, pack_p, land_p, pack_v, land_v, new, tgt, src, mom, acc, out_f, in_f, out_x, in_x, out_a, in_a,
    move_send, move_recv, x_send, x_recv, a_send, a_recv, load,
):
    grp, dom = lax.axis_index("grp"), lax.axis_index("dom")
    inner = domains.bit_length() - 1

    def partner(bit):
        return (grp, flipped(dom, bit)) if bit < inner else (flipped(grp, bit - inner), dom)

    columns = domains // 4

    def peer(step):
        return (grp, lax.rem(dom + step, domains))

    def far_first(j):
        a = lax.div(j, 4)
        along = columns // 2 + (1 - 2 * lax.rem(a, 2)) * lax.div(a + 1, 2)
        return lax.rem(j, 4) * columns + along

    barrier = pltpu.get_barrier_semaphore()
    outer = [bit for bit in bits if bit >= inner]
    land_v[:, pl.ds(6, 2)] = jnp.zeros((domains, 2, BLOCK), F32)

    def greet(j):
        pl.semaphore_signal(barrier, inc=1, device_id=peer(far_first(j)), device_id_type=MESH)

    pl.loop(0, domains - 4, unroll=10)(greet)
    for step in range(columns, domains, columns):
        pl.semaphore_signal(barrier, inc=1, device_id=peer(step), device_id_type=MESH)

    for bit in outer:
        pl.semaphore_signal(barrier, inc=1, device_id=partner(bit), device_id_type=MESH)

    loads = [
        pltpu.make_async_copy(given, held, load.at[i])
        for i, (given, held) in enumerate(((pos_in, pos), (mass_in, mass), (vel_in, vel)))
    ]
    for copy in loads:
        copy.start()

    lane = lax.broadcasted_iota(jnp.int32, (1, BLOCK), 1)
    owner = lax.rem(lane, SLOTS)
    target = jnp.zeros((1, BLOCK), jnp.int32)
    for b in range(SLOTS):
        target = jnp.where(owner == b, dest[b], target)
    rows = lax.broadcasted_iota(jnp.int32, (SLOTS, BLOCK), 0)
    lanes = lax.broadcasted_iota(jnp.int32, (SLOTS, BLOCK), 1)
    owners = lax.rem(lanes, SLOTS)

    def as_column(row):
        return jnp.sum(jnp.where(lanes == rows, row, 0.0), axis=1, keepdims=True)

    target_f = target.astype(F32)
    same = (as_column(target_f) == target_f) & (rows < owners)
    rank = jnp.sum(jnp.where(same, 1.0, 0.0), axis=0, keepdims=True)
    away = lax.rem(target - dom + domains, domains)
    away_f = away.astype(F32)
    came_from = lax.rem(dom - away + domains, domains).astype(F32) * 2.0 + rank
    place = jnp.sum(jnp.where(as_column(came_from) < came_from, 1.0, 0.0), axis=0, keepdims=True)

    def packed(stacked, stride):
        key = away_f * 8.0 + rank * stride + lax.div(lane, SLOTS).astype(F32)
        count = lax.broadcasted_iota(jnp.int32, (domains * 8, BLOCK), 0).astype(F32)
        choice = jnp.where(count == key, 1.0, 0.0).astype(BF16)
        return exact_dot(choice, stacked).reshape(domains, 8, BLOCK)

    def unpacked(land, slot, part, stride):
        rows = slot.shape[0]
        first = lax.broadcasted_iota(jnp.int32, (rows, BLOCK), 1) < SLOTS
        key = jnp.sum(jnp.where(first & (place == slot), away_f * 8.0 + rank * stride, 0.0), axis=1, keepdims=True)
        key = jnp.where(part < stride, key + part, -1.0)
        count = lax.broadcasted_iota(jnp.int32, (rows, domains * 8), 1).astype(F32)
        choice = jnp.where(count == key, 1.0, 0.0).astype(BF16)
        return exact_dot(choice, land.reshape(domains * 8, BLOCK))

    for copy in loads:
        copy.wait()
    pack_p[...] = packed(jnp.concatenate([pos[0], pos[1], pos[2], mass[...]], axis=0), 4.0)
    pl.semaphore_wait(barrier, domains - 1 + len(outer))

    def move(pack, land, k, rows):
        def send(step):
            pltpu.make_async_remote_copy(
                src_ref=pack.at[step, pl.ds(0, rows)], dst_ref=land.at[step, pl.ds(0, rows)],
                send_sem=move_send.at[k], recv_sem=move_recv.at[k],
                device_id=peer(step), device_id_type=MESH,
            ).start()

        pl.loop(0, domains - 4, unroll=10)(lambda j: send(far_first(j)))
        for step in range(columns, domains, columns):
            send(step)

    def moved(pack, land, k, rows):
        return pltpu.make_async_remote_copy(
            src_ref=pack.at[pl.ds(1, domains - 1), pl.ds(0, rows)],
            dst_ref=land.at[pl.ds(1, domains - 1), pl.ds(0, rows)],
            send_sem=move_send.at[k], recv_sem=move_recv.at[k],
            device_id=peer(1), device_id_type=MESH,
        )

    move(pack_p, land_p, 0, 8)
    pack_v[...] = packed(
        jnp.concatenate([vel[0], vel[1], vel[2], jnp.zeros((SLOTS, BLOCK), F32)], axis=0), 3.0
    )
    land_p[0] = pack_p[0]
    land_v[0] = pack_v[0]
    moved(pack_p, land_p, 0, 8).wait_recv()
    row8 = lax.broadcasted_iota(jnp.int32, (SLOTS * 8, 1), 0)
    slot8, part8 = lax.div(row8, 8).astype(F32), lax.rem(row8, 8).astype(F32)
    new[...] = unpacked(land_p[...], slot8, part8, 4.0).reshape(SLOTS, 8, BLOCK)

    def visit(r):
        return pltpu.make_async_remote_copy(
            src_ref=out_x.at[r], dst_ref=in_x.at[r], send_sem=x_send.at[r], recv_sem=x_recv.at[r],
            device_id=partner(bits[r]), device_id_type=MESH,
        )

    def give_back(r):
        return pltpu.make_async_remote_copy(
            src_ref=out_a.at[r], dst_ref=in_a.at[r], send_sem=a_send.at[r], recv_sem=a_recv.at[r],
            device_id=partner(bits[r]), device_id_type=MESH,
        )

    fetch = pltpu.make_async_remote_copy(
        src_ref=out_f, dst_ref=in_f, send_sem=x_send.at[FETCH], recv_sem=x_recv.at[FETCH],
        device_id=partner(bits[FETCH]), device_id_type=MESH,
    )
    for i in range(EXPORTS * FAR):
        out_f[i // 2, pl.ds(i % 2 * 4, 4)] = new[far_ids[i % FAR, FETCH * EXPORTS + i // FAR], pl.ds(0, 4)]
    fetch.start()
    for r in ORDER:
        for e in range(EXPORTS):
            out_x[r, e // 2, pl.ds(e % 2 * 4, 4)] = new[export_ids[e, r], pl.ds(0, 4)]
        visit(r).start()

    move(pack_v, land_v, 1, 6)

    def as_source(x, b):
        features, moments = source_rows(x)
        src[b] = jnp.concatenate([features, jnp.zeros((BLOCK - KEEP, BLOCK), F32)], axis=0).T.astype(BF16)
        mom[b] = moments

    def prepare(b, carry):
        x = new[b]
        tgt[b] = target_rows(x)
        as_source(x, b)
        return carry

    lax.fori_loop(0, SLOTS, prepare, 0, unroll=4)

    def near(b, carry):
        acc[b] = pair_sum(new[b], tgt[b], [near_ids[k, b] for k in range(NEAR)], src, mom)
        return carry

    lax.fori_loop(0, SLOTS - LATE, near, 0, unroll=10)
    for r in ORDER:
        visit(r).wait_recv()
        for e in range(EXPORTS):
            x = in_x[r, e // 2, pl.ds(e % 2 * 4, 4)]
            x = jnp.concatenate([x, jnp.zeros_like(x)], axis=0)
            ids = [far_ids[k, r * EXPORTS + e] for k in range(FAR)]
            out_a[r, e // 2, pl.ds(e % 2 * 4, 4)] = pair_sum(x, target_rows(x), ids, src, mom)[0:4]
        give_back(r).start()
    lax.fori_loop(SLOTS - LATE, SLOTS, near, 0, unroll=6)
    fetch.wait_recv()
    for i in range(EXPORTS * FAR):
        x = in_f[i // 2, pl.ds(i % 2 * 4, 4)]
        as_source(jnp.concatenate([x, jnp.zeros_like(x)], axis=0), SLOTS + i)
    for e in range(EXPORTS):
        b = export_ids[e, FETCH]
        ids = [SLOTS + e * FAR + k for k in range(FAR)]
        in_a[FETCH, e // 2, pl.ds(e % 2 * 4, 4)] = pair_sum(new[b], tgt[b], ids, src, mom)[0:4]

    moved(pack_v, land_v, 1, 6).wait_recv()
    row3 = lax.broadcasted_iota(jnp.int32, (SLOTS * 3, 1), 0)
    slot3, part3 = lax.rem(row3, SLOTS), lax.div(row3, SLOTS)
    vel_out[...] = unpacked(land_v[...], slot3.astype(F32), part3.astype(F32), 3.0).reshape(3, SLOTS, BLOCK)
    exported = jnp.full((1, BLOCK), -1, jnp.int32)
    for r in range(ROUNDS):
        if r != FETCH:
            give_back(r).wait_recv()
        for e in range(EXPORTS):
            exported = jnp.where(lax.div(lane, 4) == r * EXPORTS + e, export_ids[e, r], exported)
    hit = (slot3 == exported) & (part3 == lax.rem(lane, 4))
    returned = in_a[...].reshape(ROUNDS * EXPORTS * 4, BLOCK)
    returned = jnp.concatenate([returned, jnp.zeros((BLOCK - ROUNDS * EXPORTS * 4, BLOCK), F32)], axis=0)
    far_acc = exact_dot(jnp.where(hit, 1.0, 0.0).astype(BF16), returned).reshape(3, SLOTS, BLOCK)
    for c in range(3):
        pos_out[c] = new[:, c]
        acc_out[c] = acc[:, c] + far_acc[c]
    fetch.wait_send()
    for r in ORDER:
        visit(r).wait_send()
        give_back(r).wait_send()
    moved(pack_p, land_p, 0, 8).wait_send()
    moved(pack_v, land_v, 1, 6).wait_send()


def on_device(positions, masses, velocities, dest_dom, local_pairs, export_list, cross_pairs):
    domains = lax.axis_size("dom")
    devices = domains * lax.axis_size("grp")
    levels = devices.bit_length() - 1
    bits = [r * levels // ROUNDS for r in range(ROUNDS)]
    hbm, vmem = pl.BlockSpec(memory_space=pltpu.HBM), pl.BlockSpec(memory_space=pltpu.VMEM)
    smem = pl.BlockSpec(memory_space=pltpu.SMEM)
    moves = pltpu.VMEM((domains, 8, BLOCK), F32)
    visits = pltpu.VMEM((ROUNDS, EXPORTS // 2, 8, BLOCK), F32)
    across = (1, 0, 2)
    outs = pl.pallas_call(
        functools.partial(kernel, domains, bits),
        out_shape=(jax.ShapeDtypeStruct((3, SLOTS, BLOCK), F32),) * 3,
        in_specs=[hbm] * 3 + [smem] * 4,
        out_specs=(vmem,) * 3,
        scratch_shapes=[
            pltpu.VMEM((3, SLOTS, BLOCK), F32), pltpu.VMEM((SLOTS, BLOCK), F32), pltpu.VMEM((3, SLOTS, BLOCK), F32),
            moves, moves, moves, moves,
            pltpu.VMEM((SLOTS, 8, BLOCK), F32),
            pltpu.VMEM((SLOTS, KEEP, BLOCK), BF16),
            pltpu.VMEM((SLOTS + EXPORTS * FAR, BLOCK, BLOCK), BF16),
            pltpu.VMEM((SLOTS + EXPORTS * FAR, 32, 2 * BLOCK), BF16),
            pltpu.VMEM((SLOTS, 8, BLOCK), F32),
            pltpu.VMEM((EXPORTS * FAR // 2, 8, BLOCK), F32), pltpu.VMEM((EXPORTS * FAR // 2, 8, BLOCK), F32),
            visits, visits, visits, visits,
            pltpu.SemaphoreType.DMA((2,)), pltpu.SemaphoreType.DMA((2,)),
            pltpu.SemaphoreType.DMA((ROUNDS,)), pltpu.SemaphoreType.DMA((ROUNDS,)),
            pltpu.SemaphoreType.DMA((ROUNDS,)), pltpu.SemaphoreType.DMA((ROUNDS,)), pltpu.SemaphoreType.DMA((3,)),
        ],
        compiler_params=pltpu.CompilerParams(
            collective_id=0, has_side_effects=True, vmem_limit_bytes=60 * 2**20
        ),
    )(
        positions.transpose(across), masses, velocities.transpose(across), dest_dom,
        local_pairs.T, export_list.T, cross_pairs.T,
    )
    new_pos, new_vel, acceleration = (out.transpose(across) for out in outs)
    vel_out = new_vel + TIMESTEP * acceleration
    return new_pos + TIMESTEP * vel_out, vel_out


def solution(mesh):
    both = ("grp", "dom")
    return jax.shard_map(
        on_device,
        mesh=mesh,
        in_specs=(
            P(both, None, None), P(both, None), P(both, None, None), P(both), P(both, None), P(both, None), P(both, None),
        ),
        out_specs=(P(both, None, None), P(both, None, None)),
        check_vma=False,
    )
```

```python
import functools
import math

import jax
import jax.numpy as jnp
from jax import lax
from jax.experimental import pallas as pl
from jax.experimental.pallas import tpu as pltpu
from jax.sharding import PartitionSpec as P

BLOCK = 128
SLOTS = 32
NEAR = 4
ROUNDS = 5
EXPORTS = 4
FAR = 4
TIMESTEP = 0.5
F32, BF16 = jnp.float32, jnp.bfloat16
MESH = pl.DeviceIdType.MESH

ALPHA = 4.009245535636174
SOFT = ALPHA * 0.05**2
N0, N1, N2, N3 = 638.3696617050974, 622.7581356810975, 614.039653607777, 155.2143515804912
D0, D1 = 3.7186906578024175, 3.627694577131586
LEAD = 0.005825292410791371
SCALE = 0.01 * ALPHA**1.5 * LEAD * 2.0**SOFT
KEEP = 48
FETCH = 2
ORDER = (3, 1, 4, 0)
LATE = 12


def split3(x):
    first = x.astype(BF16).astype(F32)
    rest = x - first
    second = rest.astype(BF16).astype(F32)
    return first, second, rest - second


def exact_dot(choice, values):
    total = None
    for piece in split3(values):
        part = jnp.dot(choice, piece.astype(BF16), preferred_element_type=F32)
        total = part if total is None else total + part
    return total


def weight(t):
    v = jnp.maximum(t - SOFT, 1e-30)
    u = v * lax.rsqrt(v)
    upper = (((u + N3) * u + N2) * u + N1) * u + N0
    lower = (u + D1) * u + D0
    p = t * (lower * jnp.exp2(t))
    return upper * lax.rsqrt(p * p * t)


def target_rows(x):
    row = lax.broadcasted_iota(jnp.int32, (8, BLOCK), 0)
    x = jnp.where(row < 3, x - 0.5, 0.0)
    norm = ALPHA * jnp.sum(x * x, axis=0, keepdims=True)
    own = jnp.where(row < 3, x, jnp.where(row == 3, norm + SOFT, jnp.where(row == 4, 1.0, 0.0)))
    t1, t2, t3 = split3(own)
    return jnp.concatenate([t1, t2, t1, t2, t3, t1], axis=0).astype(BF16)


def source_rows(x):
    row = lax.broadcasted_iota(jnp.int32, (8, BLOCK), 0)
    mass = x[3:4]
    x = jnp.where(row < 3, x - 0.5, 0.0)
    norm = ALPHA * jnp.sum(x * x, axis=0, keepdims=True)
    own = jnp.where(row < 3, (-2.0 * ALPHA) * x, jnp.where(row == 3, 1.0, jnp.where(row == 4, norm, 0.0)))
    s1, s2, s3 = split3(own)
    moment = (SCALE * mass) * jnp.where(row < 3, x, jnp.where(row == 3, 1.0, 0.0))
    m1, m2, m3 = split3(moment)
    moments = jnp.concatenate([m1, m2, m3, jnp.zeros_like(m1)], axis=0).astype(BF16)
    return jnp.concatenate([s1, s1, s2, s2, s1, s3], axis=0), jnp.concatenate([moments, moments], axis=1)


def pair_sum(x, features, source_ids, src, mom):
    sources = jnp.concatenate([src[s] for s in source_ids], axis=0)[:, :KEEP]
    softened = jnp.dot(sources, features, preferred_element_type=F32)
    a = None
    for k, s in enumerate(source_ids):
        w = weight(softened[k * BLOCK : (k + 1) * BLOCK])
        high = w.astype(BF16)
        low = (w - high.astype(F32)).astype(BF16)
        part = jnp.dot(mom[s], jnp.concatenate([high, low], axis=0), preferred_element_type=F32)
        a = part if a is None else a + part
    a = a[0:8] + a[8:16] + a[16:24]
    return a - (x - 0.5) * a[3:4]


def flipped(index, bit):
    low = 2**bit
    return index + low * (1 - 2 * lax.rem(lax.div(index, low), 2))


def kernel(
    domains, bits, pos_in, mass_in, vel_in, dest, near_ids, export_ids, far_ids, pos_out, vel_out, acc_out,
    pos, mass, vel, pack_p, land_p, pack_v, land_v, pick_p, pick_v, pick_a, new, tgt, src, mom, acc, out_f, in_f, out_x, in_x, out_a, in_a,
    move_send, move_recv, x_send, x_recv, a_send, a_recv, load,
):
    grp, dom = lax.axis_index("grp"), lax.axis_index("dom")
    inner = domains.bit_length() - 1

    def partner(bit):
        return (grp, flipped(dom, bit)) if bit < inner else (flipped(grp, bit - inner), dom)

    columns = domains // 4

    def peer(step):
        there = dom + step
        return (grp, jnp.where(there >= domains, there - domains, there))

    steps = sorted(range(1, domains), key=lambda d: -min(d % columns, -d % columns))

    barrier = pltpu.get_barrier_semaphore()
    outer = [bit for bit in bits if bit >= inner]
    land_v[:, pl.ds(6, 2)] = jnp.zeros((domains, 2, BLOCK), F32)

    for step in steps:
        pl.semaphore_signal(barrier, inc=1, device_id=peer(step), device_id_type=MESH)
    for bit in outer:
        pl.semaphore_signal(barrier, inc=1, device_id=partner(bit), device_id_type=MESH)

    loads = [
        pltpu.make_async_copy(given, held, load.at[i])
        for i, (given, held) in enumerate(((pos_in, pos), (mass_in, mass), (vel_in, vel)))
    ]
    for copy in loads:
        copy.start()

    lane = lax.broadcasted_iota(jnp.int32, (1, BLOCK), 1)
    owner = lax.rem(lane, SLOTS)
    target = jnp.zeros((1, BLOCK), jnp.int32)
    for b in range(SLOTS):
        target = jnp.where(owner == b, dest[b], target)
    rows = lax.broadcasted_iota(jnp.int32, (SLOTS, BLOCK), 0)
    lanes = lax.broadcasted_iota(jnp.int32, (SLOTS, BLOCK), 1)
    owners = lax.rem(lanes, SLOTS)

    def as_column(row):
        return jnp.sum(jnp.where(lanes == rows, row, 0.0), axis=1, keepdims=True)

    target_f = target.astype(F32)
    same = (as_column(target_f) == target_f) & (rows < owners)
    rank = jnp.sum(jnp.where(same, 1.0, 0.0), axis=0, keepdims=True)
    away = lax.rem(target - dom + domains, domains)
    away_f = away.astype(F32)
    came_from = lax.rem(dom - away + domains, domains).astype(F32) * 2.0 + rank
    place = jnp.sum(jnp.where(as_column(came_from) < came_from, 1.0, 0.0), axis=0, keepdims=True)

    def packed(stacked, stride):
        key = away_f * 8.0 + rank * stride + lax.div(lane, SLOTS).astype(F32)
        count = lax.broadcasted_iota(jnp.int32, (domains * 8, BLOCK), 0).astype(F32)
        choice = jnp.where(count == key, 1.0, 0.0).astype(BF16)
        return exact_dot(choice, stacked).reshape(domains, 8, BLOCK)

    def arrivals(slot, part, stride):
        rows = slot.shape[0]
        first = lax.broadcasted_iota(jnp.int32, (rows, BLOCK), 1) < SLOTS
        key = jnp.sum(jnp.where(first & (place == slot), away_f * 8.0 + rank * stride, 0.0), axis=1, keepdims=True)
        key = jnp.where(part < stride, key + part, -1.0)
        count = lax.broadcasted_iota(jnp.int32, (rows, domains * 8), 1).astype(F32)
        return jnp.where(count == key, 1.0, 0.0).astype(BF16)

    for copy in loads:
        copy.wait()
    pack_p[...] = packed(jnp.concatenate([pos[0], pos[1], pos[2], mass[...]], axis=0), 4.0)
    pl.semaphore_wait(barrier, domains - 1 + len(outer))

    def move(pack, land, k, rows):
        for step in steps:
            pltpu.make_async_remote_copy(
                src_ref=pack.at[step, pl.ds(0, rows)], dst_ref=land.at[step, pl.ds(0, rows)],
                send_sem=move_send.at[k], recv_sem=move_recv.at[k],
                device_id=peer(step), device_id_type=MESH,
            ).start()

    def moved(pack, land, k, rows):
        return pltpu.make_async_remote_copy(
            src_ref=pack.at[pl.ds(1, domains - 1), pl.ds(0, rows)],
            dst_ref=land.at[pl.ds(1, domains - 1), pl.ds(0, rows)],
            send_sem=move_send.at[k], recv_sem=move_recv.at[k],
            device_id=peer(1), device_id_type=MESH,
        )

    move(pack_p, land_p, 0, 8)
    pack_v[...] = packed(
        jnp.concatenate([vel[0], vel[1], vel[2], jnp.zeros((SLOTS, BLOCK), F32)], axis=0), 3.0
    )
    land_p[0] = pack_p[0]
    land_v[0] = pack_v[0]
    row8 = lax.broadcasted_iota(jnp.int32, (SLOTS * 8, 1), 0)
    pick_p[...] = arrivals(lax.div(row8, 8).astype(F32), lax.rem(row8, 8).astype(F32), 4.0)
    row3 = lax.broadcasted_iota(jnp.int32, (SLOTS * 3, 1), 0)
    slot3, part3 = lax.rem(row3, SLOTS), lax.div(row3, SLOTS)
    pick_v[...] = arrivals(slot3.astype(F32), part3.astype(F32), 3.0)
    exported = jnp.full((1, BLOCK), -1, jnp.int32)
    for r in range(ROUNDS):
        for e in range(EXPORTS):
            exported = jnp.where(lax.div(lane, 4) == r * EXPORTS + e, export_ids[e, r], exported)
    hit = (slot3 == exported) & (part3 == lax.rem(lane, 4))
    pick_a[...] = jnp.where(hit, 1.0, 0.0).astype(BF16)
    moved(pack_p, land_p, 0, 8).wait_recv()
    new[...] = exact_dot(pick_p[...], land_p[...].reshape(domains * 8, BLOCK)).reshape(SLOTS, 8, BLOCK)

    def visit(r):
        return pltpu.make_async_remote_copy(
            src_ref=out_x.at[r], dst_ref=in_x.at[r], send_sem=x_send.at[r], recv_sem=x_recv.at[r],
            device_id=partner(bits[r]), device_id_type=MESH,
        )

    def give_back(r):
        return pltpu.make_async_remote_copy(
            src_ref=out_a.at[r], dst_ref=in_a.at[r], send_sem=a_send.at[r], recv_sem=a_recv.at[r],
            device_id=partner(bits[r]), device_id_type=MESH,
        )

    fetch = pltpu.make_async_remote_copy(
        src_ref=out_f, dst_ref=in_f, send_sem=x_send.at[FETCH], recv_sem=x_recv.at[FETCH],
        device_id=partner(bits[FETCH]), device_id_type=MESH,
    )
    for i in range(EXPORTS * FAR):
        out_f[i // 2, pl.ds(i % 2 * 4, 4)] = new[far_ids[i % FAR, FETCH * EXPORTS + i // FAR], pl.ds(0, 4)]
    fetch.start()
    for r in ORDER:
        for e in range(EXPORTS):
            out_x[r, e // 2, pl.ds(e % 2 * 4, 4)] = new[export_ids[e, r], pl.ds(0, 4)]
        visit(r).start()

    move(pack_v, land_v, 1, 6)

    def as_source(x, b):
        features, moments = source_rows(x)
        src[b] = jnp.concatenate([features, jnp.zeros((BLOCK - KEEP, BLOCK), F32)], axis=0).T.astype(BF16)
        mom[b] = moments

    def prepare(b, carry):
        x = new[b]
        tgt[b] = target_rows(x)
        as_source(x, b)
        return carry

    lax.fori_loop(0, SLOTS, prepare, 0, unroll=4)

    def near(b, carry):
        acc[b] = pair_sum(new[b], tgt[b], [near_ids[k, b] for k in range(NEAR)], src, mom)
        return carry

    lax.fori_loop(0, SLOTS - LATE, near, 0, unroll=10)
    @pl.loop(0, len(ORDER))
    def _(j):
        r = ORDER[0]
        for n, m in enumerate(ORDER):
            r = jnp.where(j == n, m, r)

            @pl.when(j == n)
            def _(m=m):
                visit(m).wait_recv()

        for e in range(EXPORTS):
            x = in_x[r, e // 2, pl.ds(e % 2 * 4, 4)]
            x = jnp.concatenate([x, jnp.zeros_like(x)], axis=0)
            ids = [far_ids[k, r * EXPORTS + e] for k in range(FAR)]
            out_a[r, e // 2, pl.ds(e % 2 * 4, 4)] = pair_sum(x, target_rows(x), ids, src, mom)[0:4]
        for n, m in enumerate(ORDER):

            @pl.when(j == n)
            def _(m=m):
                give_back(m).start()

    lax.fori_loop(SLOTS - LATE, SLOTS, near, 0, unroll=6)
    fetch.wait_recv()
    for i in range(EXPORTS * FAR):
        x = in_f[i // 2, pl.ds(i % 2 * 4, 4)]
        as_source(jnp.concatenate([x, jnp.zeros_like(x)], axis=0), SLOTS + i)
    for e in range(EXPORTS):
        b = export_ids[e, FETCH]
        ids = [SLOTS + e * FAR + k for k in range(FAR)]
        in_a[FETCH, e // 2, pl.ds(e % 2 * 4, 4)] = pair_sum(new[b], tgt[b], ids, src, mom)[0:4]

    for r in ORDER:
        give_back(r).wait_recv()
    returned = in_a[...].reshape(ROUNDS * EXPORTS * 4, BLOCK)
    returned = jnp.concatenate([returned, jnp.zeros((BLOCK - ROUNDS * EXPORTS * 4, BLOCK), F32)], axis=0)
    far_acc = exact_dot(pick_a[...], returned).reshape(3, SLOTS, BLOCK)
    for c in range(3):
        pos_out[c] = new[:, c]
        acc_out[c] = acc[:, c] + far_acc[c]
    moved(pack_v, land_v, 1, 6).wait_recv()
    new_vel = exact_dot(pick_v[...], land_v[...].reshape(domains * 8, BLOCK))
    vel_out[...] = new_vel.reshape(3, SLOTS, BLOCK)
    fetch.wait_send()
    for r in ORDER:
        visit(r).wait_send()
        give_back(r).wait_send()
    moved(pack_p, land_p, 0, 8).wait_send()
    moved(pack_v, land_v, 1, 6).wait_send()


def on_device(positions, masses, velocities, dest_dom, local_pairs, export_list, cross_pairs):
    domains = lax.axis_size("dom")
    devices = domains * lax.axis_size("grp")
    levels = devices.bit_length() - 1
    bits = [r * levels // ROUNDS for r in range(ROUNDS)]
    hbm, vmem = pl.BlockSpec(memory_space=pltpu.HBM), pl.BlockSpec(memory_space=pltpu.VMEM)
    smem = pl.BlockSpec(memory_space=pltpu.SMEM)
    moves = pltpu.VMEM((domains, 8, BLOCK), F32)
    visits = pltpu.VMEM((ROUNDS, EXPORTS // 2, 8, BLOCK), F32)
    across = (1, 0, 2)
    outs = pl.pallas_call(
        functools.partial(kernel, domains, bits),
        out_shape=(jax.ShapeDtypeStruct((3, SLOTS, BLOCK), F32),) * 3,
        in_specs=[hbm] * 3 + [smem] * 4,
        out_specs=(vmem,) * 3,
        scratch_shapes=[
            pltpu.VMEM((3, SLOTS, BLOCK), F32), pltpu.VMEM((SLOTS, BLOCK), F32), pltpu.VMEM((3, SLOTS, BLOCK), F32),
            moves, moves, moves, moves,
            pltpu.VMEM((SLOTS * 8, domains * 8), BF16), pltpu.VMEM((SLOTS * 3, domains * 8), BF16),
            pltpu.VMEM((SLOTS * 3, BLOCK), BF16),
            pltpu.VMEM((SLOTS, 8, BLOCK), F32),
            pltpu.VMEM((SLOTS, KEEP, BLOCK), BF16),
            pltpu.VMEM((SLOTS + EXPORTS * FAR, BLOCK, BLOCK), BF16),
            pltpu.VMEM((SLOTS + EXPORTS * FAR, 32, 2 * BLOCK), BF16),
            pltpu.VMEM((SLOTS, 8, BLOCK), F32),
            pltpu.VMEM((EXPORTS * FAR // 2, 8, BLOCK), F32), pltpu.VMEM((EXPORTS * FAR // 2, 8, BLOCK), F32),
            visits, visits, visits, visits,
            pltpu.SemaphoreType.DMA((2,)), pltpu.SemaphoreType.DMA((2,)),
            pltpu.SemaphoreType.DMA((ROUNDS,)), pltpu.SemaphoreType.DMA((ROUNDS,)),
            pltpu.SemaphoreType.DMA((ROUNDS,)), pltpu.SemaphoreType.DMA((ROUNDS,)), pltpu.SemaphoreType.DMA((3,)),
        ],
        compiler_params=pltpu.CompilerParams(
            collective_id=0, has_side_effects=True, vmem_limit_bytes=60 * 2**20
        ),
    )(
        positions.transpose(across), masses, velocities.transpose(across), dest_dom,
        local_pairs.T, export_list.T, cross_pairs.T,
    )
    new_pos, new_vel, acceleration = (out.transpose(across) for out in outs)
    vel_out = new_vel + TIMESTEP * acceleration
    return new_pos + TIMESTEP * vel_out, vel_out


def solution(mesh):
    both = ("grp", "dom")
    return jax.shard_map(
        on_device,
        mesh=mesh,
        in_specs=(
            P(both, None, None), P(both, None), P(both, None, None), P(both), P(both, None), P(both, None), P(both, None),
        ),
        out_specs=(P(both, None, None), P(both, None, None)),
        check_vma=False,
    )
```

```python
import functools
import math

import jax
import jax.numpy as jnp
from jax import lax
from jax.experimental import pallas as pl
from jax.experimental.pallas import tpu as pltpu
from jax.sharding import PartitionSpec as P

BLOCK = 128
SLOTS = 32
NEAR = 4
ROUNDS = 5
EXPORTS = 4
FAR = 4
TIMESTEP = 0.5
F32, BF16 = jnp.float32, jnp.bfloat16
MESH = pl.DeviceIdType.MESH

ALPHA = 4.009245535636174
SOFT = ALPHA * 0.05**2
N0, N1, N2, N3 = 638.3696617050974, 622.7581356810975, 614.039653607777, 155.2143515804912
D0, D1 = 3.7186906578024175, 3.627694577131586
LEAD = 0.005825292410791371
SCALE = 0.01 * ALPHA**1.5 * LEAD * 2.0**SOFT
KEEP = 48
FETCH = 2
ORDER = (3, 1, 4, 0)
LATE = 12


def split3(x):
    first = x.astype(BF16).astype(F32)
    rest = x - first
    second = rest.astype(BF16).astype(F32)
    return first, second, rest - second


def exact_dot(choice, values):
    total = None
    for piece in split3(values):
        part = jnp.dot(choice, piece.astype(BF16), preferred_element_type=F32)
        total = part if total is None else total + part
    return total


def weight(t):
    v = jnp.maximum(t - SOFT, 1e-30)
    u = v * lax.rsqrt(v)
    upper = (((u + N3) * u + N2) * u + N1) * u + N0
    lower = (u + D1) * u + D0
    p = t * (lower * jnp.exp2(t))
    return upper * lax.rsqrt(p * p * t)


def target_rows(x):
    row = lax.broadcasted_iota(jnp.int32, (8, BLOCK), 0)
    x = jnp.where(row < 3, x - 0.5, 0.0)
    norm = ALPHA * jnp.sum(x * x, axis=0, keepdims=True)
    own = jnp.where(row < 3, x, jnp.where(row == 3, norm + SOFT, jnp.where(row == 4, 1.0, 0.0)))
    t1, t2, t3 = split3(own)
    return jnp.concatenate([t1, t2, t1, t2, t3, t1], axis=0).astype(BF16)


def source_rows(x):
    row = lax.broadcasted_iota(jnp.int32, (8, BLOCK), 0)
    mass = x[3:4]
    x = jnp.where(row < 3, x - 0.5, 0.0)
    norm = ALPHA * jnp.sum(x * x, axis=0, keepdims=True)
    own = jnp.where(row < 3, (-2.0 * ALPHA) * x, jnp.where(row == 3, 1.0, jnp.where(row == 4, norm, 0.0)))
    s1, s2, s3 = split3(own)
    moment = (SCALE * mass) * jnp.where(row < 3, x, jnp.where(row == 3, 1.0, 0.0))
    m1, m2, m3 = split3(moment)
    moments = jnp.concatenate([m1, m2, m3, jnp.zeros_like(m1)], axis=0).astype(BF16)
    return jnp.concatenate([s1, s1, s2, s2, s1, s3], axis=0), jnp.concatenate([moments, moments], axis=1)


def pair_sum(x, features, source_ids, src, mom):
    sources = jnp.concatenate([src[s] for s in source_ids], axis=0)[:, :KEEP]
    softened = jnp.dot(sources, features, preferred_element_type=F32)
    a = None
    for k, s in enumerate(source_ids):
        w = weight(softened[k * BLOCK : (k + 1) * BLOCK])
        high = w.astype(BF16)
        low = (w - high.astype(F32)).astype(BF16)
        part = jnp.dot(mom[s], jnp.concatenate([high, low], axis=0), preferred_element_type=F32)
        a = part if a is None else a + part
    a = a[0:8] + a[8:16] + a[16:24]
    return a - (x - 0.5) * a[3:4]


def flipped(index, bit):
    low = 2**bit
    return index + low * (1 - 2 * lax.rem(lax.div(index, low), 2))


def kernel(
    domains, bits, pos_in, mass_in, vel_in, dest, near_ids, export_ids, far_ids, pos_out, vel_out, acc_out,
    pos, mass, vel, pack_p, land_p, pack_v, land_v, pick_p, pick_v, pick_a, new, tgt, src, mom, acc, out_f, in_f, out_x, in_x, out_a, in_a,
    move_send, move_recv, x_send, x_recv, a_send, a_recv, load,
):
    grp, dom = lax.axis_index("grp"), lax.axis_index("dom")
    inner = domains.bit_length() - 1

    def partner(bit):
        return (grp, flipped(dom, bit)) if bit < inner else (flipped(grp, bit - inner), dom)

    columns = domains // 4

    def peer(step):
        there = dom + step
        return (grp, jnp.where(there >= domains, there - domains, there))

    steps = sorted(range(1, domains), key=lambda d: -min(d % columns, -d % columns))

    barrier = pltpu.get_barrier_semaphore()
    outer = [bit for bit in bits if bit >= inner]
    land_v[:, pl.ds(6, 2)] = jnp.zeros((domains, 2, BLOCK), F32)

    for step in steps:
        pl.semaphore_signal(barrier, inc=1, device_id=peer(step), device_id_type=MESH)
    for bit in outer:
        pl.semaphore_signal(barrier, inc=1, device_id=partner(bit), device_id_type=MESH)

    loads = [
        pltpu.make_async_copy(given, held, load.at[i])
        for i, (given, held) in enumerate(((pos_in, pos), (mass_in, mass), (vel_in, vel)))
    ]
    for copy in loads:
        copy.start()

    lane = lax.broadcasted_iota(jnp.int32, (1, BLOCK), 1)
    owner = lax.rem(lane, SLOTS)
    target = jnp.zeros((1, BLOCK), jnp.int32)
    for b in range(SLOTS):
        target = jnp.where(owner == b, dest[b], target)
    rows = lax.broadcasted_iota(jnp.int32, (SLOTS, BLOCK), 0)
    lanes = lax.broadcasted_iota(jnp.int32, (SLOTS, BLOCK), 1)
    owners = lax.rem(lanes, SLOTS)

    def as_column(row):
        return jnp.sum(jnp.where(lanes == rows, row, 0.0), axis=1, keepdims=True)

    target_f = target.astype(F32)
    same = (as_column(target_f) == target_f) & (rows < owners)
    rank = jnp.sum(jnp.where(same, 1.0, 0.0), axis=0, keepdims=True)
    away = lax.rem(target - dom + domains, domains)
    away_f = away.astype(F32)
    came_from = lax.rem(dom - away + domains, domains).astype(F32) * 2.0 + rank
    place = jnp.sum(jnp.where(as_column(came_from) < came_from, 1.0, 0.0), axis=0, keepdims=True)

    def packed(stacked, stride):
        key = away_f * 8.0 + rank * stride + lax.div(lane, SLOTS).astype(F32)
        count = lax.broadcasted_iota(jnp.int32, (domains * 8, BLOCK), 0).astype(F32)
        choice = jnp.where(count == key, 1.0, 0.0).astype(BF16)
        return exact_dot(choice, stacked).reshape(domains, 8, BLOCK)

    def arrivals(slot, part, stride):
        rows = slot.shape[0]
        first = lax.broadcasted_iota(jnp.int32, (rows, BLOCK), 1) < SLOTS
        key = jnp.sum(jnp.where(first & (place == slot), away_f * 8.0 + rank * stride, 0.0), axis=1, keepdims=True)
        key = jnp.where(part < stride, key + part, -1.0)
        count = lax.broadcasted_iota(jnp.int32, (rows, domains * 8), 1).astype(F32)
        return jnp.where(count == key, 1.0, 0.0).astype(BF16)

    for copy in loads[:2]:
        copy.wait()
    pack_p[...] = packed(jnp.concatenate([pos[0], pos[1], pos[2], mass[...]], axis=0), 4.0)
    pl.semaphore_wait(barrier, domains - 1 + len(outer))

    def move(pack, land, k, rows):
        for step in steps:
            pltpu.make_async_remote_copy(
                src_ref=pack.at[step, pl.ds(0, rows)], dst_ref=land.at[step, pl.ds(0, rows)],
                send_sem=move_send.at[k], recv_sem=move_recv.at[k],
                device_id=peer(step), device_id_type=MESH,
            ).start()

    def moved(pack, land, k, rows):
        return pltpu.make_async_remote_copy(
            src_ref=pack.at[pl.ds(1, domains - 1), pl.ds(0, rows)],
            dst_ref=land.at[pl.ds(1, domains - 1), pl.ds(0, rows)],
            send_sem=move_send.at[k], recv_sem=move_recv.at[k],
            device_id=peer(1), device_id_type=MESH,
        )

    move(pack_p, land_p, 0, 8)
    loads[2].wait()
    pack_v[...] = packed(
        jnp.concatenate([vel[0], vel[1], vel[2], jnp.zeros((SLOTS, BLOCK), F32)], axis=0), 3.0
    )
    land_p[0] = pack_p[0]
    land_v[0] = pack_v[0]
    row8 = lax.broadcasted_iota(jnp.int32, (SLOTS * 8, 1), 0)
    pick_p[...] = arrivals(lax.div(row8, 8).astype(F32), lax.rem(row8, 8).astype(F32), 4.0)
    row3 = lax.broadcasted_iota(jnp.int32, (SLOTS * 3, 1), 0)
    slot3, part3 = lax.rem(row3, SLOTS), lax.div(row3, SLOTS)
    pick_v[...] = arrivals(slot3.astype(F32), part3.astype(F32), 3.0)
    exported = jnp.full((1, BLOCK), -1, jnp.int32)
    for r in range(ROUNDS):
        for e in range(EXPORTS):
            exported = jnp.where(lax.div(lane, 4) == r * EXPORTS + e, export_ids[e, r], exported)
    hit = (slot3 == exported) & (part3 == lax.rem(lane, 4))
    pick_a[...] = jnp.where(hit, 1.0, 0.0).astype(BF16)
    moved(pack_p, land_p, 0, 8).wait_recv()
    new[...] = exact_dot(pick_p[...], land_p[...].reshape(domains * 8, BLOCK)).reshape(SLOTS, 8, BLOCK)

    def visit(r):
        return pltpu.make_async_remote_copy(
            src_ref=out_x.at[r], dst_ref=in_x.at[r], send_sem=x_send.at[r], recv_sem=x_recv.at[r],
            device_id=partner(bits[r]), device_id_type=MESH,
        )

    def give_back(r):
        return pltpu.make_async_remote_copy(
            src_ref=out_a.at[r], dst_ref=in_a.at[r], send_sem=a_send.at[r], recv_sem=a_recv.at[r],
            device_id=partner(bits[r]), device_id_type=MESH,
        )

    fetch = pltpu.make_async_remote_copy(
        src_ref=out_f, dst_ref=in_f, send_sem=x_send.at[FETCH], recv_sem=x_recv.at[FETCH],
        device_id=partner(bits[FETCH]), device_id_type=MESH,
    )
    for i in range(EXPORTS * FAR):
        out_f[i // 2, pl.ds(i % 2 * 4, 4)] = new[far_ids[i % FAR, FETCH * EXPORTS + i // FAR], pl.ds(0, 4)]
    fetch.start()
    for r in ORDER:
        for e in range(EXPORTS):
            out_x[r, e // 2, pl.ds(e % 2 * 4, 4)] = new[export_ids[e, r], pl.ds(0, 4)]
        visit(r).start()

    move(pack_v, land_v, 1, 6)

    def as_source(x, b):
        features, moments = source_rows(x)
        src[b] = jnp.concatenate([features, jnp.zeros((BLOCK - KEEP, BLOCK), F32)], axis=0).T.astype(BF16)
        mom[b] = moments

    def prepare(b, carry):
        x = new[b]
        tgt[b] = target_rows(x)
        as_source(x, b)
        return carry

    lax.fori_loop(0, SLOTS, prepare, 0, unroll=4)

    def near(b, carry):
        acc[b] = pair_sum(new[b], tgt[b], [near_ids[k, b] for k in range(NEAR)], src, mom)
        return carry

    lax.fori_loop(0, SLOTS - LATE, near, 0, unroll=10)
    @pl.loop(0, len(ORDER))
    def _(j):
        r = ORDER[0]
        for n, m in enumerate(ORDER):
            r = jnp.where(j == n, m, r)

            @pl.when(j == n)
            def _(m=m):
                visit(m).wait_recv()

        for e in range(EXPORTS):
            x = in_x[r, e // 2, pl.ds(e % 2 * 4, 4)]
            x = jnp.concatenate([x, jnp.zeros_like(x)], axis=0)
            ids = [far_ids[k, r * EXPORTS + e] for k in range(FAR)]
            out_a[r, e // 2, pl.ds(e % 2 * 4, 4)] = pair_sum(x, target_rows(x), ids, src, mom)[0:4]
        for n, m in enumerate(ORDER):

            @pl.when(j == n)
            def _(m=m):
                give_back(m).start()

    lax.fori_loop(SLOTS - LATE, SLOTS, near, 0, unroll=6)
    fetch.wait_recv()
    for i in range(EXPORTS * FAR):
        x = in_f[i // 2, pl.ds(i % 2 * 4, 4)]
        as_source(jnp.concatenate([x, jnp.zeros_like(x)], axis=0), SLOTS + i)
    for e in range(EXPORTS):
        b = export_ids[e, FETCH]
        ids = [SLOTS + e * FAR + k for k in range(FAR)]
        in_a[FETCH, e // 2, pl.ds(e % 2 * 4, 4)] = pair_sum(new[b], tgt[b], ids, src, mom)[0:4]

    for r in ORDER:
        give_back(r).wait_recv()
    returned = in_a[...].reshape(ROUNDS * EXPORTS * 4, BLOCK)
    returned = jnp.concatenate([returned, jnp.zeros((BLOCK - ROUNDS * EXPORTS * 4, BLOCK), F32)], axis=0)
    far_acc = exact_dot(pick_a[...], returned).reshape(3, SLOTS, BLOCK)
    for c in range(3):
        pos_out[c] = new[:, c]
        acc_out[c] = acc[:, c] + far_acc[c]
    moved(pack_v, land_v, 1, 6).wait_recv()
    new_vel = exact_dot(pick_v[...], land_v[...].reshape(domains * 8, BLOCK))
    vel_out[...] = new_vel.reshape(3, SLOTS, BLOCK)
    fetch.wait_send()
    for r in ORDER:
        visit(r).wait_send()
        give_back(r).wait_send()
    moved(pack_p, land_p, 0, 8).wait_send()
    moved(pack_v, land_v, 1, 6).wait_send()


def on_device(positions, masses, velocities, dest_dom, local_pairs, export_list, cross_pairs):
    domains = lax.axis_size("dom")
    devices = domains * lax.axis_size("grp")
    levels = devices.bit_length() - 1
    bits = [r * levels // ROUNDS for r in range(ROUNDS)]
    hbm, vmem = pl.BlockSpec(memory_space=pltpu.HBM), pl.BlockSpec(memory_space=pltpu.VMEM)
    smem = pl.BlockSpec(memory_space=pltpu.SMEM)
    moves = pltpu.VMEM((domains, 8, BLOCK), F32)
    visits = pltpu.VMEM((ROUNDS, EXPORTS // 2, 8, BLOCK), F32)
    across = (1, 0, 2)
    outs = pl.pallas_call(
        functools.partial(kernel, domains, bits),
        out_shape=(jax.ShapeDtypeStruct((3, SLOTS, BLOCK), F32),) * 3,
        in_specs=[hbm] * 3 + [smem] * 4,
        out_specs=(vmem,) * 3,
        scratch_shapes=[
            pltpu.VMEM((3, SLOTS, BLOCK), F32), pltpu.VMEM((SLOTS, BLOCK), F32), pltpu.VMEM((3, SLOTS, BLOCK), F32),
            moves, moves, moves, moves,
            pltpu.VMEM((SLOTS * 8, domains * 8), BF16), pltpu.VMEM((SLOTS * 3, domains * 8), BF16),
            pltpu.VMEM((SLOTS * 3, BLOCK), BF16),
            pltpu.VMEM((SLOTS, 8, BLOCK), F32),
            pltpu.VMEM((SLOTS, KEEP, BLOCK), BF16),
            pltpu.VMEM((SLOTS + EXPORTS * FAR, BLOCK, BLOCK), BF16),
            pltpu.VMEM((SLOTS + EXPORTS * FAR, 32, 2 * BLOCK), BF16),
            pltpu.VMEM((SLOTS, 8, BLOCK), F32),
            pltpu.VMEM((EXPORTS * FAR // 2, 8, BLOCK), F32), pltpu.VMEM((EXPORTS * FAR // 2, 8, BLOCK), F32),
            visits, visits, visits, visits,
            pltpu.SemaphoreType.DMA((2,)), pltpu.SemaphoreType.DMA((2,)),
            pltpu.SemaphoreType.DMA((ROUNDS,)), pltpu.SemaphoreType.DMA((ROUNDS,)),
            pltpu.SemaphoreType.DMA((ROUNDS,)), pltpu.SemaphoreType.DMA((ROUNDS,)), pltpu.SemaphoreType.DMA((3,)),
        ],
        compiler_params=pltpu.CompilerParams(
            collective_id=0, has_side_effects=True, vmem_limit_bytes=60 * 2**20
        ),
    )(
        positions.transpose(across), masses, velocities.transpose(across), dest_dom,
        local_pairs.T, export_list.T, cross_pairs.T,
    )
    new_pos, new_vel, acceleration = (out.transpose(across) for out in outs)
    vel_out = new_vel + TIMESTEP * acceleration
    return new_pos + TIMESTEP * vel_out, vel_out


def solution(mesh):
    both = ("grp", "dom")
    return jax.shard_map(
        on_device,
        mesh=mesh,
        in_specs=(
            P(both, None, None), P(both, None), P(both, None, None), P(both), P(both, None), P(both, None), P(both, None),
        ),
        out_specs=(P(both, None, None), P(both, None, None)),
        check_vma=False,
    )
```
